32 devices in a mesh: groups: 2 (over x), aux: 16 (over z, y, core).
Axes of the slice: x: 2, y: 2, z: 4, core: 2. Of those that a mesh axis runs over, the one named last changes fastest.
Arguments:
- blocks: bfloat16 [4096, 4096], P(('groups', 'aux')), parts along dimension 0, may hold values from -0.29882812 to 0.29882812
- right_xform: bfloat16 [4096, 4096], P(('groups', 'aux')), parts along dimension 0, may hold values from -0.59765625 to 0.59765625
- left_xform: bfloat16 [4096, 4096], P(('groups', 'aux')), parts along dimension 0, may hold values from -0.59765625 to 0.59765625
- owner: int32 [4096, 1], P(('groups', 'aux')), parts along dimension 0, may hold values from 0 to 15; in each aligned block of 128 rows (0 to 127, 128 to 255, ...) at most 16 rows name the same one
- tile_slot: int32 [4096], P(('groups', 'aux')), parts along dimension 0, may hold values from 0 to 7
- domain: int32 [4096], P(('groups', 'aux')), parts along dimension 0, may hold values from 0 to 2
- live_count: int32 [32], P(('groups', 'aux')), parts along dimension 0, may hold values from 1 to 128, 1536 in all
- right_vec: float32 [16384], P(('groups', 'aux')), parts along dimension 0, may hold values from -6 to 6
- left_vec: float32 [16384], P(('groups', 'aux')), parts along dimension 0, may hold values from -6 to 6
- occ_energy: float32 [8], P('groups'), parts along dimension 0, may hold values from -0.56 to -0.5
- vir_energy: float32 [4096], P('groups'), parts along dimension 0, may hold values from 0.5 to 3
- omega: float32 [2], P('groups'), parts along dimension 0, may hold values from 1.78 to 1.85
Outputs:
- sigma_right: float32 [16384], P(('groups', 'aux')), parts along dimension 0
- sigma_left: float32 [16384], P(('groups', 'aux')), parts along dimension 0
The draws below stay inside these ranges and needn't reach their ends.
There are 2 independent parts, one for each index of `groups`. The reference program is written for one: setup_inputs(seed, part) draws one part's arguments, and reference() takes and returns one part's arrays. A program takes and returns all parts, laid end to end along the dimension named above; each array names one. Nothing has to cross between parts.
Inputs may be any that keep to these rules, and one draw needn't show every extreme that they name: Among the 128 blocks of one aux device at most 16 share an owner, and on some device exactly 16 do. `live_count`: the counts sum to 1536 and some device has all 128 blocks live; blocks at or past the count are ignored.
All inputs are finite; a program needn't handle non-finite values.
Results may differ from the reference program's by a relative error of at most 0.0024.
Values may be sent and summed in bfloat16 or wider, within the bound.
A program may use at most 128 MiB of HBM per device.

```python
import math
import jax
import jax.numpy as jnp
import numpy as np
from jax import lax

BLK = 64
NVIR = 2048
ADOM_DEV = 3
TILE_DEV = 8
NB_DEV = 128
NDOM = 48
NAUX = 3072
NTILE = 128
OV = 8192
NOCCW = 4
NB_TOTAL = 2048
CAP = 16
N_AUX = 16


def draw_vir_energy(key, part):
    key = jax.random.fold_in(key, 7)
    pick_key, lower_key, upper_key = jax.random.split(key, 3)
    lower_band = jax.random.bernoulli(pick_key, 0.15, (NVIR,))
    lower_values = jax.random.uniform(lower_key, (NVIR,), jnp.float32, 0.5, 0.56)
    upper_values = jax.random.uniform(upper_key, (NVIR,), jnp.float32, 0.56, 3.0)
    return jnp.where(lower_band, lower_values, upper_values)


def set_ends(array, stream_key, smallest, high):
    extent = array.shape
    place = [jax.random.randint(jax.random.fold_in(stream_key, axis), (), 0, extent[axis]) for axis in range(len(extent))]
    array = array.at[tuple(place)].set(smallest)
    longest = extent.index(max(extent))
    place[longest] = (place[longest] + 1) % extent[longest]
    return array.at[tuple(place)].set(high)


def block_levels(key, dims, cuts, least, largest):
    factor_of = 1.0
    for position, shards_of in cuts:
        heights = jax.random.uniform(jax.random.fold_in(jax.random.fold_in(key, 6), position), (shards_of,), jnp.float32, least / len(cuts), largest / len(cuts))
        factor_of = factor_of * jnp.repeat(jnp.exp(heights), dims[position] // shards_of).reshape((-1,) + (1,) * (len(dims) - 1 - position))
    return factor_of


def length_profile(number_of, total, most, skew):
    loads = [(1 << 20) // math.isqrt(rank ** skew) + 1 for rank in range(2, number_of + 1)]
    surplus, given = total - most - (number_of - 1), [1] * (number_of - 1)
    while surplus > 0:
        free = [i for i in range(number_of - 1) if given[i] < most]
        mass, left = sum([loads[i] for i in free]), surplus
        for i in free:
            more = min(most - given[i], max(1, left * loads[i] // mass), surplus)
            given[i] = given[i] + more
            surplus = surplus - more
    return np.array([most] + given)


def ragged_sizes(key, number_of, total, reach, slope):
    if number_of == 2:
        one = jax.random.randint(key, (), max(1, total - reach), min(reach, total - 1) + 1)
        return jnp.stack([one, total - one])
    sizes = jnp.asarray(length_profile(number_of, total, reach, slope), jnp.int32)
    twos = (number_of - 1) // 2
    giver, taker = sizes[1:1 + 2 * twos:2], sizes[2:2 + 2 * twos:2]
    room = jnp.minimum(giver - 1, reach - taker)
    passed = jax.random.randint(jax.random.fold_in(key, 1), (twos,), 0, 1 << 20) % (room + 1)
    sizes = sizes.at[1:1 + 2 * twos:2].set(giver - passed).at[2:2 + 2 * twos:2].set(taker + passed)
    return sizes[jax.random.permutation(jax.random.fold_in(key, 2), number_of)]


def routed_block(own_key, own, number, rows, number_of, top, most, skew):
    sequence = jax.random.permutation(own_key, number_of)
    packed, usual = load_shares(number_of, rows * top, most, skew, True), load_shares(number_of, rows * top, most, skew, False)
    places = jnp.arange(number_of)

    def named(lengths, rotation):
        used = int((lengths > 0).sum())
        fixed = max(1, used // 4)
        passed = fixed + (places - fixed + rotation * (used - fixed)) % max(1, number_of - fixed)
        return jnp.zeros((number_of,), jnp.int32).at[sequence[jnp.where(places < fixed, places, passed)]].set(jnp.asarray(lengths, jnp.int32))

    lengths = jnp.where(number % 4 == 0, named(packed, number // 4), named(usual, number - number // 4 - 1))
    mixed = jax.random.permutation(jax.random.fold_in(own, 3), number_of)
    donor, taker = mixed[0:number_of // 2 * 2:2], mixed[1:number_of // 2 * 2:2]
    room = jnp.minimum(lengths[donor] - 1, most - lengths[taker]) // 2
    room = jnp.where((donor == sequence[0]) | (taker == sequence[0]) | (lengths[taker] == 0), 0, jnp.maximum(room, 0))
    passed = jax.random.randint(jax.random.fold_in(own, 4), (number_of // 2,), 0, 1 << 20) % (room + 1)
    lengths = lengths.at[donor].add(-passed).at[taker].add(passed)
    labels = jnp.searchsorted(jnp.cumsum(lengths), jnp.arange(rows * top), side="right").astype(jnp.int32)
    table = labels.reshape(top, rows).T
    table = table[jax.random.permutation(jax.random.fold_in(own, 1), rows)]
    rotation = jax.random.randint(jax.random.fold_in(own, 2), (rows, 1), 0, top)
    return jnp.take_along_axis(table, (jnp.arange(top)[None, :] + rotation) % top, axis=1)


def load_shares(number_of, total, limit, slope, full):
    portions = [(1 << 20) // math.isqrt(standing ** slope) + 1 for standing in range(1, number_of + 1)]
    largest = limit if full else min(limit, max(-(-total // number_of), total * portions[0] // sum(portions)))
    least = 1 if total - largest >= number_of - 1 else 0
    holding, spare = [largest] + [least] * (number_of - 1), total - largest - least * (number_of - 1)
    while spare > 0:
        movable = [i for i in range(1, number_of) if holding[i] < largest] or [i for i in range(1, number_of) if holding[i] < limit]
        mass, left = sum([portions[i] for i in movable]), spare
        for i in movable:
            more = min(limit - holding[i], max(1, left * portions[i] // mass), spare)
            holding[i] = holding[i] + more
            spare = spare - more
    return np.array(holding)


def scatter_about(key, dims, spread, reach, shards=(), kind=jnp.bfloat16):
    drawn = spread * jax.random.normal(key, dims, jnp.float32)
    if shards:
        drawn = drawn * block_levels(key, dims, shards, -0.22, 0.18)
    return jnp.clip(drawn, -reach, reach).astype(kind)


def setup_inputs(seed: int = 0, part: int = 0) -> dict:
    splits = jax.random.split(jax.random.key(seed), 13)
    part_keys = jax.random.split(jax.random.fold_in(splits[12], part), 13)
    blocks = scatter_about(part_keys[0], (NB_TOTAL, BLK * BLK), 0.05, 0.29882812, ((0, 16),))
    right_xform = scatter_about(part_keys[1], (NB_TOTAL, BLK * BLK), 0.1, 0.59765625, ((0, 16),))
    left_xform = scatter_about(part_keys[2], (NB_TOTAL, BLK * BLK), 0.1, 0.59765625, ((0, 16),))
    owner_keys = jax.random.split(jax.random.fold_in(part_keys[3], 1), NB_TOTAL // NB_DEV)
    owner_turns = jax.random.permutation(jax.random.fold_in(part_keys[3], 3), NB_TOTAL // NB_DEV)
    owner = jax.vmap(lambda own, number: routed_block(jax.random.fold_in(part_keys[3], 2), own, number, NB_DEV, N_AUX, 1, CAP, 2))(owner_keys, owner_turns).reshape((NB_TOTAL, 1))
    tile_slot = set_ends(jax.random.randint(part_keys[4], (NB_TOTAL,), 0, TILE_DEV), jax.random.fold_in(part_keys[4], 1), 0, TILE_DEV - 1).astype(jnp.int32)
    domain = set_ends(jax.random.randint(part_keys[5], (NB_TOTAL,), 0, ADOM_DEV), jax.random.fold_in(part_keys[5], 1), 0, ADOM_DEV - 1).astype(jnp.int32)
    live_count = ragged_sizes(part_keys[6], N_AUX, 3 * NB_DEV * N_AUX // 4, NB_DEV, 2).astype(jnp.int32)
    right_vec = scatter_about(part_keys[7], (OV,), 1.0, 6.0, ((0, 16),), jnp.float32)
    left_vec = scatter_about(part_keys[8], (OV,), 1.0, 6.0, ((0, 16),), jnp.float32)
    occ_energy = jnp.clip(jax.random.uniform(part_keys[9], (NOCCW,), jnp.float32, -0.56, -0.5), -0.56, -0.5)
    vir_energy = draw_vir_energy(jax.random.fold_in(jax.random.fold_in(splits[12], part), 71), part)
    omega = jnp.clip(jax.random.uniform(part_keys[11], (1,), jnp.float32, 1.78, 1.85), 1.78, 1.85)
    return {"blocks": blocks, "right_xform": right_xform, "left_xform": left_xform, "owner": owner, "tile_slot": tile_slot, "domain": domain, "live_count": live_count, "right_vec": right_vec, "left_vec": left_vec, "occ_energy": occ_energy, "vir_energy": vir_energy, "omega": omega}


def reference(blocks, right_xform, left_xform, owner, tile_slot, domain, live_count, right_vec, left_vec, occ_energy, vir_energy, omega):
    stacked = jnp.stack([blocks, right_xform, left_xform], axis=1).reshape(NB_TOTAL, 3, BLK, BLK)
    block_ids = jnp.arange(NB_TOTAL, dtype=jnp.int32)
    holder = block_ids // NB_DEV
    is_live = (block_ids % NB_DEV) < live_count[holder]
    global_dom = holder * ADOM_DEV + domain
    target = owner[:, 0]
    global_tile = target * TILE_DEV + tile_slot
    masked3 = jnp.where(is_live[:, None, None, None], stacked, jnp.zeros_like(stacked)).astype(jnp.float32)
    masked = masked3[:, 0]
    trials = jnp.stack([right_vec, left_vec]).astype(jnp.bfloat16)
    trials = lax.optimization_barrier(trials).astype(jnp.float32)
    picked = trials.reshape(2, NTILE, BLK)[:, global_tile, :]
    contrib = jnp.einsum('brc,kbc->kbr', masked, picked, precision=lax.Precision.HIGHEST)
    coulomb = jnp.stack([jax.ops.segment_sum(contrib[0], global_dom, num_segments=NDOM),
                         jax.ops.segment_sum(contrib[1], global_dom, num_segments=NDOM)]).reshape(2, NAUX)
    pair_ids = jnp.arange(OV, dtype=jnp.int32)
    energy_gap = vir_energy[pair_ids % NVIR] - occ_energy[pair_ids // NVIR]
    own_pairs = TILE_DEV * BLK

    def per_owner(device):
        take = is_live & (target == device)
        segment_ids = jnp.where(take, tile_slot * NDOM + global_dom, TILE_DEV * NDOM)
        slab3 = jax.ops.segment_sum(masked3, segment_ids, num_segments=TILE_DEV * NDOM + 1)[:-1]
        slab3 = slab3.reshape(TILE_DEV, NDOM, 3, BLK, BLK).transpose(2, 1, 3, 0, 4).reshape(3, NAUX, own_pairs)
        slab = slab3[0]
        rounded = slab.astype(jnp.bfloat16)
        xform_r = slab3[1].astype(jnp.bfloat16)
        xform_l = slab3[2].astype(jnp.bfloat16)
        cross_r = jnp.dot(rounded.T, xform_r, preferred_element_type=jnp.float32)
        cross_l = jnp.dot(rounded.T, xform_l, preferred_element_type=jnp.float32)
        gram_r = cross_r + cross_r.T
        start = (device * own_pairs).astype(jnp.int32)
        right_part = lax.dynamic_slice_in_dim(right_vec, start, own_pairs)
        left_part = lax.dynamic_slice_in_dim(left_vec, start, own_pairs)
        gaps = lax.dynamic_slice_in_dim(energy_gap, start, own_pairs)
        coulomb_term = jnp.dot(coulomb, slab, precision=lax.Precision.HIGHEST)
        denominator = omega[0] - gaps[:, None] - gaps[None, :]
        sigma_r = gaps * right_part + coulomb_term[0] + jnp.dot(gram_r / denominator, right_part, precision=lax.Precision.HIGHEST)
        sigma_l = gaps * left_part + coulomb_term[1] + jnp.dot(cross_l / denominator, left_part, precision=lax.Precision.HIGHEST)
        return sigma_r, sigma_l

    sigma_r, sigma_l = lax.map(per_owner, jnp.arange(N_AUX, dtype=jnp.int32))
    return sigma_r.reshape(OV), sigma_l.reshape(OV)
```

```python
import functools

import jax
import jax.numpy as jnp
from jax import lax
from jax.experimental import pallas as pl
from jax.experimental.pallas import tpu as pltpu
from jax.sharding import PartitionSpec as P

BLK = 64
NVIR = 2048
ADOM_DEV = 3
LANES = 128
F32 = jnp.float32
BF16 = jnp.bfloat16


def kernel(
    n,
    group,
    occ_ref,
    omega_ref,
    code_ref,
    blocks_ref,
    right_ref,
    left_ref,
    trial_ref,
    vir_ref,
    out_ref,
    b_slab,
    r_slab,
    l_slab,
    vir_col,
    w_right,
    w_left,
    y_ref,
    trials,
    share,
    arrived,
    gather_send,
    gather_recv,
    share_send,
    share_recv,
):
    me = lax.axis_index("aux")
    pairs = w_right.shape[0]
    lane_tiles = pairs // LANES
    rows_of_slab = ADOM_DEV * lane_tiles
    sub = BLK * BLK // LANES
    slab_rows = ADOM_DEV * BLK
    hot_rows = group * rows_of_slab

    def peer(step):
        return lax.rem(me + 1 + step, n)

    barrier = pltpu.get_barrier_semaphore()

    def greet(step, carry):
        pl.semaphore_signal(barrier, inc=1, device_id={"aux": peer(step)})
        return carry

    lax.fori_loop(0, n - 1, greet, 0)
    pl.semaphore_wait(barrier, n - 1)

    def gather_copy(target, source):
        return pltpu.make_async_remote_copy(
            src_ref=trial_ref,
            dst_ref=trials.at[source],
            send_sem=gather_send.at[target],
            recv_sem=gather_recv.at[source],
            device_id={"aux": target},
        )

    def share_copy(target, source):
        return pltpu.make_async_remote_copy(
            src_ref=share.at[target],
            dst_ref=arrived.at[source],
            send_sem=share_send.at[target],
            recv_sem=share_recv.at[source],
            device_id={"aux": target},
        )

    def start_gather(step, carry):
        gather_copy(peer(step), me).start()
        return carry

    lax.fori_loop(0, n - 1, start_gather, 0)
    trials[me] = trial_ref[...]

    for i in range(NVIR // LANES):
        row = jnp.broadcast_to(vir_ref[i : i + 1, :], (LANES, LANES))
        vir_col[i * LANES : (i + 1) * LANES, :] = row.T

    def assemble(source_ref, slab, base, g):
        slot = lax.broadcasted_iota(jnp.int32, (hot_rows, code_ref.shape[1]), 0)
        hot = jnp.where(slot + g * hot_rows == code_ref[...], 1.0, 0.0).astype(BF16)
        low = lax.broadcasted_iota(jnp.int32, (source_ref.shape[0], LANES), 1) < BLK

        def chunk(j, carry):
            straight, crossed = [], []
            for half in range(2):
                x = source_ref[:, pl.ds(pl.multiple_of(j * 2 * LANES + half * LANES, LANES), LANES)]
                x = x.astype(F32)
                turned = pltpu.roll(x, BLK, 1)
                zero = jnp.zeros_like(x)
                straight.append(
                    jnp.concatenate([jnp.where(low, x, zero), jnp.where(low, zero, turned)], 0)
                )
                crossed.append(
                    jnp.concatenate([jnp.where(low, turned, zero), jnp.where(low, zero, x)], 0)
                )
            for parity, parts in enumerate((straight, crossed)):
                z = jnp.concatenate(parts, 1).astype(BF16)
                placed = jnp.dot(hot, z, preferred_element_type=F32)
                for half in range(2):
                    slab[parity, pl.ds(base + j * 2 + half, hot_rows, stride=sub), :] = placed[
                        :, half * LANES : (half + 1) * LANES
                    ]
            return carry

        lax.fori_loop(0, sub // 2, chunk, 0)

    def lane_tile(slab, s, t):
        parts = []
        for d in range(ADOM_DEV):
            for parity in range(2):
                first = (s * rows_of_slab + d * lane_tiles + t) * sub
                parts.append(slab[parity, pl.ds(pl.multiple_of(first, sub), sub), :])
        return jnp.concatenate(parts, 0)

    for g in range(n // group):
        assemble(blocks_ref, b_slab, g * hot_rows * sub, g)

    def wait_gather(step, carry):
        gather_copy(peer(step), peer(step)).wait_recv()
        return carry

    lax.fori_loop(0, n - 1, wait_gather, 0)

    def add_y(s, state):
        acc_r, acc_l = state
        vec = trials[s].astype(BF16).astype(F32)
        for t in range(lane_tiles):
            tile = lane_tile(b_slab, s, t)
            acc_r = acc_r + tile * vec[t : t + 1, :]
            acc_l = acc_l + tile * vec[lane_tiles + t : lane_tiles + t + 1, :]
        return acc_r, acc_l

    zero = jnp.zeros((slab_rows, LANES), F32)
    acc_r, acc_l = lax.fori_loop(0, n, add_y, (zero, zero))
    y_ref[0] = jnp.broadcast_to(jnp.sum(acc_r, 1, keepdims=True), (slab_rows, LANES))
    y_ref[1] = jnp.broadcast_to(jnp.sum(acc_l, 1, keepdims=True), (slab_rows, LANES))

    per_occ = NVIR // pairs
    nt = (((1,), (1,)), ((), ()))

    for g in range(n // group):
        assemble(right_ref, r_slab, 0, g)
        assemble(left_ref, l_slab, 0, g)

        def slab_step(step, carry):
            local = lax.rem(me + 1 + step, group)
            s = g * group + local
            shift = omega_ref[0] + 2.0 * occ_ref[s // per_occ]
            part = lax.rem(s, per_occ)
            column = vir_col[pl.ds(pl.multiple_of(part * pairs, pairs), pairs), :]
            energies = vir_ref[pl.ds(part * lane_tiles, lane_tiles), :]
            vec = trials[s]
            for t in range(lane_tiles):
                lanes = slice(t * LANES, (t + 1) * LANES)
                inverse = pl.reciprocal((shift - energies[t : t + 1, :]) - column, approx=True)
                w_right[:, lanes] = (inverse * vec[t : t + 1, :]).astype(BF16)
                w_left[:, lanes] = (
                    inverse * vec[lane_tiles + t : lane_tiles + t + 1, :]
                ).astype(BF16)
            b = jnp.concatenate([lane_tile(b_slab, s, t) for t in range(lane_tiles)], 1)
            x_r = jnp.concatenate([lane_tile(r_slab, local, t) for t in range(lane_tiles)], 1)
            x_l = jnp.concatenate([lane_tile(l_slab, local, t) for t in range(lane_tiles)], 1)
            b16, r16 = b.astype(BF16), x_r.astype(BF16)
            t_r = lax.dot_general(r16, w_right[...], nt, preferred_element_type=F32)
            t_b = lax.dot_general(b16, w_right[...], nt, preferred_element_type=F32)
            t_l = lax.dot_general(x_l.astype(BF16), w_left[...], nt, preferred_element_type=F32)
            y_r = jnp.concatenate([y_ref[0]] * lane_tiles, 1)
            y_l = jnp.concatenate([y_ref[1]] * lane_tiles, 1)
            sig_r = jnp.sum(b * (t_r + y_r) + x_r * t_b, 0, keepdims=True)
            sig_l = jnp.sum(b * (t_l + y_l), 0, keepdims=True)
            for t in range(lane_tiles):
                lanes = slice(t * LANES, (t + 1) * LANES)
                share[s, t : t + 1, :] = sig_r[:, lanes]
                share[s, lane_tiles + t : lane_tiles + t + 1, :] = sig_l[:, lanes]

            @pl.when(s != me)
            def _():
                share_copy(s, me).start()

            return carry

        lax.fori_loop(0, group, slab_step, 0)

    own = lax.rem(me, per_occ)
    energies = vir_ref[pl.ds(own * lane_tiles, lane_tiles), :] - occ_ref[me // per_occ]
    total = jnp.concatenate([energies, energies], 0) * trial_ref[...] + share[me]

    def collect(step, total):
        source = peer(step)
        share_copy(source, source).wait_recv()
        return total + arrived[source]

    out_ref[...] = lax.fori_loop(0, n - 1, collect, total)

    def wait_sent(step, carry):
        gather_copy(peer(step), me).wait_send()
        share_copy(peer(step), me).wait_send()
        return carry

    lax.fori_loop(0, n - 1, wait_sent, 0)


def on_device(
    blocks,
    right_xform,
    left_xform,
    owner,
    tile_slot,
    domain,
    live_count,
    right_vec,
    left_vec,
    occ_energy,
    vir_energy,
    omega,
):
    n = lax.axis_size("aux")
    nb_local, flat_width = blocks.shape
    pairs = right_vec.shape[0]
    lane_tiles = pairs // LANES
    group = min(n, 16)
    is_live = jnp.arange(nb_local, dtype=jnp.int32) < live_count[0]
    slot = (owner[:, 0] * ADOM_DEV + domain) * lane_tiles + tile_slot // 2
    code = jnp.concatenate(
        [jnp.where(is_live & (tile_slot % 2 == half), slot, -1) for half in range(2)]
    )[None, :]
    trial = jnp.concatenate([right_vec, left_vec]).reshape(2 * lane_tiles, LANES)
    vir = vir_energy.reshape(NVIR // LANES, LANES)
    sub = flat_width // LANES
    slab = group * ADOM_DEV * lane_tiles * sub
    vmem, smem = (
        pl.BlockSpec(memory_space=pltpu.VMEM),
        pl.BlockSpec(memory_space=pltpu.SMEM),
    )
    out = pl.pallas_call(
        functools.partial(kernel, n, group),
        out_shape=jax.ShapeDtypeStruct((2 * lane_tiles, LANES), F32),
        in_specs=[smem, smem] + [vmem] * 6,
        out_specs=vmem,
        scratch_shapes=[
            pltpu.VMEM((2, slab * (n // group), LANES), F32),
            pltpu.VMEM((2, slab, LANES), F32),
            pltpu.VMEM((2, slab, LANES), F32),
            pltpu.VMEM((NVIR, LANES), F32),
            pltpu.VMEM((pairs, pairs), BF16),
            pltpu.VMEM((pairs, pairs), BF16),
            pltpu.VMEM((2, ADOM_DEV * BLK, LANES), F32),
            pltpu.VMEM((n, 2 * lane_tiles, LANES), F32),
            pltpu.VMEM((n, 2 * lane_tiles, LANES), F32),
            pltpu.VMEM((n, 2 * lane_tiles, LANES), F32),
            pltpu.SemaphoreType.DMA((n,)),
            pltpu.SemaphoreType.DMA((n,)),
            pltpu.SemaphoreType.DMA((n,)),
            pltpu.SemaphoreType.DMA((n,)),
        ],
        compiler_params=pltpu.CompilerParams(
            collective_id=0, has_side_effects=True, vmem_limit_bytes=56 * 1024 * 1024
        ),
    )(occ_energy, omega, code, blocks, right_xform, left_xform, trial, vir)
    return out[:lane_tiles].reshape(pairs), out[lane_tiles:].reshape(pairs)


def solution(mesh):
    in_specs = (
        P(("groups", "aux"), None),
        P(("groups", "aux"), None),
        P(("groups", "aux"), None),
        P(("groups", "aux"), None),
        P(("groups", "aux")),
        P(("groups", "aux")),
        P(("groups", "aux")),
        P(("groups", "aux")),
        P(("groups", "aux")),
        P("groups"),
        P("groups"),
        P("groups"),
    )
    out_specs = (P(("groups", "aux")), P(("groups", "aux")))
    return jax.shard_map(
        on_device, mesh=mesh, in_specs=in_specs, out_specs=out_specs, check_vma=False
    )
```

```python
import functools

import jax
import jax.numpy as jnp
from jax import lax
from jax.experimental import pallas as pl
from jax.experimental.pallas import tpu as pltpu
from jax.sharding import PartitionSpec as P

BLK = 64
NVIR = 2048
ADOM_DEV = 3
LANES = 128
F32 = jnp.float32
BF16 = jnp.bfloat16


def kernel(
    n,
    occ_ref,
    omega_ref,
    block_of_ref,
    code_row_ref,
    code_col_ref,
    blocks_ref,
    right_ref,
    left_ref,
    trial_ref,
    vir_ref,
    out_ref,
    turned,
    b_straight,
    b_crossed,
    r_straight,
    r_crossed,
    l_straight,
    l_crossed,
    vir_col,
    w_right,
    w_left,
    y_ref,
    trials,
    share,
    arrived,
    gather_send,
    gather_recv,
    share_send,
    share_recv,
):
    me = lax.axis_index("aux")
    pairs = w_right.shape[0]
    lane_tiles = pairs // LANES
    tiles = 2 * lane_tiles
    sub = BLK * BLK // LANES
    slab_rows = ADOM_DEV * BLK
    nb = blocks_ref.shape[0]
    pitch = turned.shape[0] // nb

    def peer(step):
        return lax.rem(me + 1 + step, n)

    barrier = pltpu.get_barrier_semaphore()

    def greet(step, carry):
        pl.semaphore_signal(barrier, inc=1, device_id={"aux": peer(step)})
        return carry

    lax.fori_loop(0, n - 1, greet, 0)

    for i in range(NVIR // LANES):
        row = jnp.broadcast_to(vir_ref[i : i + 1, :], (LANES, LANES))
        vir_col[i * LANES : (i + 1) * LANES, :] = row.T

    pl.semaphore_wait(barrier, n - 1)

    def gather_copy(target, source):
        return pltpu.make_async_remote_copy(
            src_ref=trial_ref,
            dst_ref=trials.at[source],
            send_sem=gather_send.at[target],
            recv_sem=gather_recv.at[source],
            device_id={"aux": target},
        )

    def share_copy(target, source):
        return pltpu.make_async_remote_copy(
            src_ref=share.at[target],
            dst_ref=arrived.at[source],
            send_sem=share_send.at[target],
            recv_sem=share_recv.at[source],
            device_id={"aux": target},
        )

    def start_gather(step, carry):
        gather_copy(peer(step), me).start()
        return carry

    lax.fori_loop(0, n - 1, start_gather, 0)
    trials[me] = trial_ref[...]

    same = jnp.where(code_col_ref[...] == code_row_ref[...], 1.0, 0.0).astype(BF16)

    def assemble(source_ref, straight, crossed):
        def chunk(j, carry):
            first = pl.multiple_of(j * 2 * LANES, 2 * LANES)
            merged = jnp.dot(
                same, source_ref[:, pl.ds(first, 2 * LANES)], preferred_element_type=F32
            )
            for half in range(2):
                turned[pl.ds(j * 2 + half, nb, stride=pitch), :] = merged[
                    :, half * LANES : (half + 1) * LANES
                ]
            return carry

        lax.fori_loop(0, sub // 2, chunk, 0)

        def settle(i, carry):
            for k in range(8):
                b = i * 8 + k
                x = turned[pl.ds(pl.multiple_of(b * pitch, 8), sub), :]
                straight[b] = x.astype(BF16)
                crossed[b] = pltpu.roll(x, BLK, 1).astype(BF16)
            return carry

        lax.fori_loop(0, nb // 8, settle, 0)
        straight[nb] = jnp.zeros((sub, LANES), BF16)
        crossed[nb] = jnp.zeros((sub, LANES), BF16)

    low = lax.broadcasted_iota(jnp.int32, (sub, LANES), 1) < BLK

    def lane_tile(straight, crossed, s, t):
        parts = []
        for d in range(ADOM_DEV):
            slot = s * (ADOM_DEV * tiles) + d * tiles + 2 * t
            first, second = block_of_ref[slot], block_of_ref[slot + 1]
            parts.append(jnp.where(low, straight[first], crossed[second]))
            parts.append(jnp.where(low, crossed[first], straight[second]))
        return jnp.concatenate(parts, 0)

    assemble(blocks_ref, b_straight, b_crossed)
    assemble(right_ref, r_straight, r_crossed)
    assemble(left_ref, l_straight, l_crossed)

    def wait_gather(step, carry):
        gather_copy(peer(step), peer(step)).wait_recv()
        return carry

    lax.fori_loop(0, n - 1, wait_gather, 0)

    def add_y(s, state):
        acc_r, acc_l = state
        vec = trials[s].astype(BF16).astype(F32)
        for t in range(lane_tiles):
            tile = lane_tile(b_straight, b_crossed, s, t).astype(F32)
            acc_r = acc_r + tile * vec[t : t + 1, :]
            acc_l = acc_l + tile * vec[lane_tiles + t : lane_tiles + t + 1, :]
        return acc_r, acc_l

    zero = jnp.zeros((slab_rows, LANES), F32)
    acc_r, acc_l = lax.fori_loop(0, n, add_y, (zero, zero))
    y_ref[0] = jnp.broadcast_to(jnp.sum(acc_r, 1, keepdims=True), (slab_rows, LANES))
    y_ref[1] = jnp.broadcast_to(jnp.sum(acc_l, 1, keepdims=True), (slab_rows, LANES))

    per_occ = NVIR // pairs

    def slab_step(step, carry):
        s = peer(step)
        shift = omega_ref[0] + 2.0 * occ_ref[s // per_occ]
        part = lax.rem(s, per_occ)
        column = vir_col[pl.ds(pl.multiple_of(part * pairs, pairs), pairs), :]
        energies = vir_ref[pl.ds(part * lane_tiles, lane_tiles), :]
        vec = trials[s].T
        col_r, col_l = [
            jnp.concatenate(
                [
                    jnp.broadcast_to(vec[:, k : k + 1], (LANES, LANES))
                    for k in range(first, first + lane_tiles)
                ],
                0,
            )
            for first in (0, lane_tiles)
        ]
        for t in range(lane_tiles):
            lanes = slice(t * LANES, (t + 1) * LANES)
            inverse = pl.reciprocal((shift - energies[t : t + 1, :]) - column, approx=True)
            w_right[:, lanes] = (inverse * col_r).astype(BF16)
            w_left[:, lanes] = (inverse * col_l).astype(BF16)
        b = jnp.concatenate(
            [lane_tile(b_straight, b_crossed, s, t) for t in range(lane_tiles)], 1
        )
        x_r = jnp.concatenate(
            [lane_tile(r_straight, r_crossed, s, t) for t in range(lane_tiles)], 1
        )
        x_l = jnp.concatenate(
            [lane_tile(l_straight, l_crossed, s, t) for t in range(lane_tiles)], 1
        )
        both = jnp.dot(
            jnp.concatenate([x_r, b], 0), w_right[...], preferred_element_type=F32
        )
        t_r, t_b = both[:slab_rows], both[slab_rows:]
        t_l = jnp.dot(x_l, w_left[...], preferred_element_type=F32)
        y_r = jnp.concatenate([y_ref[0]] * lane_tiles, 1)
        y_l = jnp.concatenate([y_ref[1]] * lane_tiles, 1)
        b = b.astype(F32)
        sig_r = jnp.sum(b * (t_r + y_r) + x_r.astype(F32) * t_b, 0, keepdims=True)
        sig_l = jnp.sum(b * (t_l + y_l), 0, keepdims=True)
        for t in range(lane_tiles):
            lanes = slice(t * LANES, (t + 1) * LANES)
            share[s, t : t + 1, :] = sig_r[:, lanes]
            share[s, lane_tiles + t : lane_tiles + t + 1, :] = sig_l[:, lanes]

        @pl.when(step < n - 1)
        def _():
            share_copy(s, me).start()

        return carry

    lax.fori_loop(0, n, slab_step, 0)

    own = lax.rem(me, per_occ)
    energies = vir_ref[pl.ds(own * lane_tiles, lane_tiles), :] - occ_ref[me // per_occ]
    total = jnp.concatenate([energies, energies], 0) * trial_ref[...] + share[me]

    def collect(step, total):
        source = peer(step)
        share_copy(source, source).wait_recv()
        return total + arrived[source]

    out_ref[...] = lax.fori_loop(0, n - 1, collect, total)

    def wait_sent(step, carry):
        gather_copy(peer(step), me).wait_send()
        share_copy(peer(step), me).wait_send()
        return carry

    lax.fori_loop(0, n - 1, wait_sent, 0)


def on_device(
    blocks,
    right_xform,
    left_xform,
    owner,
    tile_slot,
    domain,
    live_count,
    right_vec,
    left_vec,
    occ_energy,
    vir_energy,
    omega,
):
    n = lax.axis_size("aux")
    nb_local, flat_width = blocks.shape
    pairs = right_vec.shape[0]
    lane_tiles = pairs // LANES
    tiles = 2 * lane_tiles
    is_live = jnp.arange(nb_local, dtype=jnp.int32) < live_count[0]
    code = jnp.where(is_live, (owner[:, 0] * ADOM_DEV + domain) * tiles + tile_slot, -1)
    slots = jnp.arange(n * ADOM_DEV * tiles, dtype=jnp.int32)
    block_of = jnp.min(
        jnp.where(
            code[None, :] == slots[:, None], jnp.arange(nb_local, dtype=jnp.int32)[None, :], nb_local
        ),
        axis=1,
    )
    trial = jnp.concatenate([right_vec, left_vec]).reshape(2 * lane_tiles, LANES)
    vir = vir_energy.reshape(NVIR // LANES, LANES)
    sub = flat_width // LANES
    vmem, smem = (
        pl.BlockSpec(memory_space=pltpu.VMEM),
        pl.BlockSpec(memory_space=pltpu.SMEM),
    )
    out = pl.pallas_call(
        functools.partial(kernel, n),
        out_shape=jax.ShapeDtypeStruct((2 * lane_tiles, LANES), F32),
        in_specs=[smem] * 3 + [vmem] * 7,
        out_specs=vmem,
        scratch_shapes=[
            pltpu.VMEM((nb_local * (sub + 8), LANES), F32),
            *[pltpu.VMEM((nb_local + 1, sub, LANES), BF16)] * 6,
            pltpu.VMEM((NVIR, LANES), F32),
            pltpu.VMEM((pairs, pairs), BF16),
            pltpu.VMEM((pairs, pairs), BF16),
            pltpu.VMEM((2, ADOM_DEV * BLK, LANES), F32),
            pltpu.VMEM((n, 2 * lane_tiles, LANES), F32),
            pltpu.VMEM((n, 2 * lane_tiles, LANES), F32),
            pltpu.VMEM((n, 2 * lane_tiles, LANES), F32),
            pltpu.SemaphoreType.DMA((n,)),
            pltpu.SemaphoreType.DMA((n,)),
            pltpu.SemaphoreType.DMA((n,)),
            pltpu.SemaphoreType.DMA((n,)),
        ],
        compiler_params=pltpu.CompilerParams(
            collective_id=0, has_side_effects=True, vmem_limit_bytes=56 * 1024 * 1024
        ),
    )(occ_energy, omega, block_of, code[None, :], code[:, None], blocks, right_xform, left_xform, trial, vir)
    return out[:lane_tiles].reshape(pairs), out[lane_tiles:].reshape(pairs)


def solution(mesh):
    in_specs = (
        P(("groups", "aux"), None),
        P(("groups", "aux"), None),
        P(("groups", "aux"), None),
        P(("groups", "aux"), None),
        P(("groups", "aux")),
        P(("groups", "aux")),
        P(("groups", "aux")),
        P(("groups", "aux")),
        P(("groups", "aux")),
        P("groups"),
        P("groups"),
        P("groups"),
    )
    out_specs = (P(("groups", "aux")), P(("groups", "aux")))
    return jax.shard_map(
        on_device, mesh=mesh, in_specs=in_specs, out_specs=out_specs, check_vma=False
    )
```

```python
import functools

import jax
import jax.numpy as jnp
from jax import lax
from jax.experimental import pallas as pl
from jax.experimental.pallas import tpu as pltpu
from jax.sharding import PartitionSpec as P

BLK = 64
NVIR = 2048
ADOM_DEV = 3
LANES = 128
WIDE = 8
F32 = jnp.float32
BF16 = jnp.bfloat16


def kernel(
    n,
    occ_ref,
    omega_ref,
    block_of_ref,
    code_row_ref,
    code_col_ref,
    blocks_ref,
    right_ref,
    left_ref,
    trial_ref,
    vir_ref,
    out_ref,
    turned_b,
    turned_r,
    turned_l,
    b_straight,
    b_crossed,
    r_straight,
    r_crossed,
    l_straight,
    l_crossed,
    vir_col,
    w_right0,
    w_left0,
    w_right1,
    w_left1,
    y_ref,
    trials,
    share,
    arrived,
    gather_send,
    gather_recv,
    share_send,
    share_recv,
):
    me = lax.axis_index("aux")
    pairs = w_right0.shape[0]
    lane_tiles = pairs // LANES
    tiles = 2 * lane_tiles
    sub = BLK * BLK // LANES
    slab_rows = ADOM_DEV * BLK
    nb = blocks_ref.shape[0]
    pitch = turned_b.shape[0] // nb

    def peer(step):
        return lax.rem(me + 1 + step, n)

    barrier = pltpu.get_barrier_semaphore()

    def greet(step, carry):
        pl.semaphore_signal(barrier, inc=1, device_id={"aux": peer(step)})
        return carry

    lax.fori_loop(0, n - 1, greet, 0)

    for i in range(NVIR // LANES):
        row = jnp.broadcast_to(vir_ref[i : i + 1, :], (LANES, LANES))
        vir_col[i * LANES : (i + 1) * LANES, :] = row.T

    pl.semaphore_wait(barrier, n - 1)

    def gather_copy(target, source):
        return pltpu.make_async_remote_copy(
            src_ref=trial_ref,
            dst_ref=trials.at[source],
            send_sem=gather_send.at[target],
            recv_sem=gather_recv.at[source],
            device_id={"aux": target},
        )

    def share_copy(target, source):
        return pltpu.make_async_remote_copy(
            src_ref=share.at[target],
            dst_ref=arrived.at[source],
            send_sem=share_send.at[target],
            recv_sem=share_recv.at[source],
            device_id={"aux": target},
        )

    def start_gather(step, carry):
        gather_copy(peer(step), me).start()
        return carry

    lax.fori_loop(0, n - 1, start_gather, 0)
    trials[me] = trial_ref[...]

    same = jnp.where(code_col_ref[...] == code_row_ref[...], 1.0, 0.0).astype(BF16)

    arrays = (
        (blocks_ref, turned_b, b_straight, b_crossed),
        (right_ref, turned_r, r_straight, r_crossed),
        (left_ref, turned_l, l_straight, l_crossed),
    )

    def merge(j, carry):
        first = pl.multiple_of(j * WIDE * LANES, WIDE * LANES)
        for source_ref, turned, _, _ in arrays:
            merged = jnp.dot(
                same, source_ref[:, pl.ds(first, WIDE * LANES)], preferred_element_type=F32
            )
            for k in range(WIDE):
                turned[pl.ds(j * WIDE + k, nb, stride=pitch), :] = merged[
                    :, k * LANES : (k + 1) * LANES
                ]
        return carry

    lax.fori_loop(0, sub // WIDE, merge, 0)

    def settle(i, carry):
        for _, turned, straight, crossed in arrays:
            for k in range(4):
                b = i * 4 + k
                x = turned[pl.ds(pl.multiple_of(b * pitch, 8), sub), :]
                straight[b] = x.astype(BF16)
                crossed[b] = pltpu.roll(x, BLK, 1).astype(BF16)
        return carry

    lax.fori_loop(0, nb // 4, settle, 0)
    for _, _, straight, crossed in arrays:
        straight[nb] = jnp.zeros((sub, LANES), BF16)
        crossed[nb] = jnp.zeros((sub, LANES), BF16)

    low = lax.broadcasted_iota(jnp.int32, (sub, LANES), 1) < BLK

    def lane_tile(straight, crossed, s, t):
        parts = []
        for d in range(ADOM_DEV):
            slot = s * (ADOM_DEV * tiles) + d * tiles + 2 * t
            first, second = block_of_ref[slot], block_of_ref[slot + 1]
            parts.append(jnp.where(low, straight[first], crossed[second]))
            parts.append(jnp.where(low, crossed[first], straight[second]))
        return jnp.concatenate(parts, 0)

    def wait_gather(step, carry):
        gather_copy(peer(step), peer(step)).wait_recv()
        return carry

    lax.fori_loop(0, n - 1, wait_gather, 0)

    def add_y(s, state):
        acc_r, acc_l = state
        vec = trials[s].astype(BF16).astype(F32)
        for t in range(lane_tiles):
            tile = lane_tile(b_straight, b_crossed, s, t).astype(F32)
            acc_r = acc_r + tile * vec[t : t + 1, :]
            acc_l = acc_l + tile * vec[lane_tiles + t : lane_tiles + t + 1, :]
        return acc_r, acc_l

    zero = jnp.zeros((slab_rows, LANES), F32)
    acc_r, acc_l = lax.fori_loop(0, n, add_y, (zero, zero))
    y_ref[0] = jnp.broadcast_to(jnp.sum(acc_r, 1, keepdims=True), (slab_rows, LANES))
    y_ref[1] = jnp.broadcast_to(jnp.sum(acc_l, 1, keepdims=True), (slab_rows, LANES))

    per_occ = NVIR // pairs

    def weights(s, w_right, w_left):
        shift = omega_ref[0] + 2.0 * occ_ref[s // per_occ]
        part = lax.rem(s, per_occ)
        column = vir_col[pl.ds(pl.multiple_of(part * pairs, pairs), pairs), :]
        energies = vir_ref[pl.ds(part * lane_tiles, lane_tiles), :]
        vec = trials[s].T
        col_r, col_l = [
            jnp.concatenate(
                [
                    jnp.broadcast_to(vec[:, k : k + 1], (LANES, LANES))
                    for k in range(first, first + lane_tiles)
                ],
                0,
            )
            for first in (0, lane_tiles)
        ]
        for t in range(lane_tiles):
            lanes = slice(t * LANES, (t + 1) * LANES)
            inverse = pl.reciprocal((shift - energies[t : t + 1, :]) - column, approx=True)
            w_right[:, lanes] = (inverse * col_r).astype(BF16)
            w_left[:, lanes] = (inverse * col_l).astype(BF16)

    def slab_term(s, w_right, w_left):
        b, x_r, x_l = [
            jnp.concatenate([lane_tile(straight, crossed, s, t) for t in range(lane_tiles)], 1)
            for _, _, straight, crossed in arrays
        ]
        both = jnp.dot(
            jnp.concatenate([x_r, b], 0), w_right[...], preferred_element_type=F32
        )
        t_r, t_b = both[:slab_rows], both[slab_rows:]
        t_l = jnp.dot(x_l, w_left[...], preferred_element_type=F32)
        y_r = jnp.concatenate([y_ref[0]] * lane_tiles, 1)
        y_l = jnp.concatenate([y_ref[1]] * lane_tiles, 1)
        b = b.astype(F32)
        sig_r = jnp.sum(b * (t_r + y_r) + x_r.astype(F32) * t_b, 0, keepdims=True)
        sig_l = jnp.sum(b * (t_l + y_l), 0, keepdims=True)
        for t in range(lane_tiles):
            lanes = slice(t * LANES, (t + 1) * LANES)
            share[s, t : t + 1, :] = sig_r[:, lanes]
            share[s, lane_tiles + t : lane_tiles + t + 1, :] = sig_l[:, lanes]

    weights(peer(0), w_right0, w_left0)

    def two_slabs(i, carry):
        weights(peer(2 * i + 1), w_right1, w_left1)
        slab_term(peer(2 * i), w_right0, w_left0)
        weights(peer(2 * i + 2), w_right0, w_left0)
        slab_term(peer(2 * i + 1), w_right1, w_left1)
        share_copy(peer(2 * i), me).start()

        @pl.when(2 * i + 1 < n - 1)
        def _():
            share_copy(peer(2 * i + 1), me).start()

        return carry

    lax.fori_loop(0, n // 2, two_slabs, 0)

    own = lax.rem(me, per_occ)
    energies = vir_ref[pl.ds(own * lane_tiles, lane_tiles), :] - occ_ref[me // per_occ]
    total = jnp.concatenate([energies, energies], 0) * trial_ref[...] + share[me]

    def collect(step, total):
        source = peer(step)
        share_copy(source, source).wait_recv()
        return total + arrived[source]

    out_ref[...] = lax.fori_loop(0, n - 1, collect, total)

    def wait_sent(step, carry):
        gather_copy(peer(step), me).wait_send()
        share_copy(peer(step), me).wait_send()
        return carry

    lax.fori_loop(0, n - 1, wait_sent, 0)


def on_device(
    blocks,
    right_xform,
    left_xform,
    owner,
    tile_slot,
    domain,
    live_count,
    right_vec,
    left_vec,
    occ_energy,
    vir_energy,
    omega,
):
    n = lax.axis_size("aux")
    nb_local, flat_width = blocks.shape
    pairs = right_vec.shape[0]
    lane_tiles = pairs // LANES
    tiles = 2 * lane_tiles
    is_live = jnp.arange(nb_local, dtype=jnp.int32) < live_count[0]
    code = jnp.where(is_live, (owner[:, 0] * ADOM_DEV + domain) * tiles + tile_slot, -1)
    slots = jnp.arange(n * ADOM_DEV * tiles, dtype=jnp.int32)
    block_of = jnp.min(
        jnp.where(
            code[None, :] == slots[:, None], jnp.arange(nb_local, dtype=jnp.int32)[None, :], nb_local
        ),
        axis=1,
    )
    trial = jnp.concatenate([right_vec, left_vec]).reshape(2 * lane_tiles, LANES)
    vir = vir_energy.reshape(NVIR // LANES, LANES)
    sub = flat_width // LANES
    vmem, smem = (
        pl.BlockSpec(memory_space=pltpu.VMEM),
        pl.BlockSpec(memory_space=pltpu.SMEM),
    )
    out = pl.pallas_call(
        functools.partial(kernel, n),
        out_shape=jax.ShapeDtypeStruct((2 * lane_tiles, LANES), F32),
        in_specs=[smem] * 3 + [vmem] * 7,
        out_specs=vmem,
        scratch_shapes=[
            *[pltpu.VMEM((nb_local * (sub + 8), LANES), F32)] * 3,
            *[pltpu.VMEM((nb_local + 1, sub, LANES), BF16)] * 6,
            pltpu.VMEM((NVIR, LANES), F32),
            *[pltpu.VMEM((pairs, pairs), BF16)] * 4,
            pltpu.VMEM((2, ADOM_DEV * BLK, LANES), F32),
            pltpu.VMEM((n, 2 * lane_tiles, LANES), F32),
            pltpu.VMEM((n, 2 * lane_tiles, LANES), F32),
            pltpu.VMEM((n, 2 * lane_tiles, LANES), F32),
            pltpu.SemaphoreType.DMA((n,)),
            pltpu.SemaphoreType.DMA((n,)),
            pltpu.SemaphoreType.DMA((n,)),
            pltpu.SemaphoreType.DMA((n,)),
        ],
        compiler_params=pltpu.CompilerParams(
            collective_id=0, has_side_effects=True, vmem_limit_bytes=56 * 1024 * 1024
        ),
    )(occ_energy, omega, block_of, code[None, :], code[:, None], blocks, right_xform, left_xform, trial, vir)
    return out[:lane_tiles].reshape(pairs), out[lane_tiles:].reshape(pairs)


def solution(mesh):
    in_specs = (
        P(("groups", "aux"), None),
        P(("groups", "aux"), None),
        P(("groups", "aux"), None),
        P(("groups", "aux"), None),
        P(("groups", "aux")),
        P(("groups", "aux")),
        P(("groups", "aux")),
        P(("groups", "aux")),
        P(("groups", "aux")),
        P("groups"),
        P("groups"),
        P("groups"),
    )
    out_specs = (P(("groups", "aux")), P(("groups", "aux")))
    return jax.shard_map(
        on_device, mesh=mesh, in_specs=in_specs, out_specs=out_specs, check_vma=False
    )
```

```python
import functools

import jax
import jax.numpy as jnp
from jax import lax
from jax.experimental import pallas as pl
from jax.experimental.pallas import tpu as pltpu
from jax.sharding import PartitionSpec as P

BLK = 64
NVIR = 2048
ADOM_DEV = 3
LANES = 128
WIDE = 8
PART = 2
F32 = jnp.float32
BF16 = jnp.bfloat16


def kernel(
    n,
    occ_ref,
    omega_ref,
    live_ref,
    owner_ref,
    slot_ref,
    domain_ref,
    blocks_hbm,
    right_hbm,
    left_hbm,
    right_vec_ref,
    left_vec_ref,
    vir_ref,
    out_ref,
    blocks_ref,
    right_ref,
    left_ref,
    load_sem,
    table,
    block_of_ref,
    table_sem,
    trial_ref,
    turned_b,
    turned_r,
    turned_l,
    b_straight,
    b_crossed,
    r_straight,
    r_crossed,
    l_straight,
    l_crossed,
    vir_col,
    w_right0,
    w_left0,
    w_right1,
    w_left1,
    y_ref,
    trials,
    share,
    arrived,
    gather_send,
    gather_recv,
    share_send,
    share_recv,
):
    me = lax.axis_index("aux")
    pairs = w_right0.shape[0]
    lane_tiles = pairs // LANES
    tiles = 2 * lane_tiles
    sub = BLK * BLK // LANES
    slab_rows = ADOM_DEV * BLK
    nb = blocks_ref.shape[0]
    pitch = turned_b.shape[0] // nb

    def peer(step):
        return lax.rem(me + 1 + step, n)

    barrier = pltpu.get_barrier_semaphore()

    def greet(step, carry):
        pl.semaphore_signal(barrier, inc=1, device_id={"aux": peer(step)})
        return carry

    loads = [
        pltpu.make_async_copy(source, target, load_sem.at[k])
        for k, (source, target) in enumerate(
            ((blocks_hbm, blocks_ref), (right_hbm, right_ref), (left_hbm, left_ref))
        )
    ]
    for load in loads:
        load.start()
    lax.fori_loop(0, n - 1, greet, 0)

    trial_ref[:lane_tiles, :] = right_vec_ref[...]
    trial_ref[lane_tiles:, :] = left_vec_ref[...]
    trials[me] = trial_ref[...]

    live = lax.broadcasted_iota(jnp.int32, (1, nb), 1) < live_ref[...]
    code = (owner_ref[...] * ADOM_DEV + domain_ref[...]) * tiles + slot_ref[...]
    code = jnp.where(live, code, -1).astype(F32)
    code_row = jnp.broadcast_to(code, (nb, nb))
    code_col = code_row.T
    same = jnp.where(code_col == code_row, 1.0, 0.0).astype(BF16)
    block_ids = lax.broadcasted_iota(jnp.int32, (nb, LANES), 0)
    lane_ids = lax.broadcasted_iota(jnp.int32, (nb, LANES), 1)

    def fill(s, carry):
        slots = (lane_ids + s * (ADOM_DEV * tiles)).astype(F32)
        held = jnp.where(code_col[:, :LANES] == slots, block_ids, nb)
        table[pl.ds(s, 1), :] = jnp.min(held, 0, keepdims=True)
        return carry

    lax.fori_loop(0, n, fill, 0)
    to_scalars = pltpu.make_async_copy(table, block_of_ref, table_sem)
    to_scalars.start()

    for i in range(NVIR // LANES):
        row = jnp.broadcast_to(vir_ref[i : i + 1, :], (LANES, LANES))
        vir_col[i * LANES : (i + 1) * LANES, :] = row.T

    def gather_copy(target, source):
        return pltpu.make_async_remote_copy(
            src_ref=trial_ref,
            dst_ref=trials.at[source],
            send_sem=gather_send.at[target],
            recv_sem=gather_recv.at[source],
            device_id={"aux": target},
        )

    def share_copy(target, source):
        return pltpu.make_async_remote_copy(
            src_ref=share.at[target],
            dst_ref=arrived.at[source],
            send_sem=share_send.at[target],
            recv_sem=share_recv.at[source],
            device_id={"aux": target},
        )

    def start_gather(step, carry):
        gather_copy(peer(step), me).start()
        return carry

    arrays = (
        (blocks_ref, turned_b, b_straight, b_crossed),
        (right_ref, turned_r, r_straight, r_crossed),
        (left_ref, turned_l, l_straight, l_crossed),
    )

    def merge(j, carry):
        first = pl.multiple_of(j * WIDE * LANES, WIDE * LANES)
        for source_ref, turned, _, _ in arrays:
            merged = jnp.dot(
                same, source_ref[:, pl.ds(first, WIDE * LANES)], preferred_element_type=F32
            )
            for k in range(WIDE):
                turned[pl.ds(j * WIDE + k, nb, stride=pitch), :] = merged[
                    :, k * LANES : (k + 1) * LANES
                ]
        return carry

    for load in loads:
        load.wait()
    lax.fori_loop(0, sub // WIDE, merge, 0)
    pl.semaphore_wait(barrier, n - 1)
    lax.fori_loop(0, n - 1, start_gather, 0)

    def settle(i, carry):
        for _, turned, straight, crossed in arrays:
            for k in range(4):
                b = i * 4 + k
                x = turned[pl.ds(pl.multiple_of(b * pitch, 8), sub), :]
                x = x.astype(BF16)
                straight[b] = x
                crossed[b] = jnp.concatenate([x[:, BLK:], x[:, :BLK]], 1)
        return carry

    lax.fori_loop(0, nb // 4, settle, 0)
    for _, _, straight, crossed in arrays:
        straight[nb] = jnp.zeros((sub, LANES), BF16)
        crossed[nb] = jnp.zeros((sub, LANES), BF16)

    low = lax.broadcasted_iota(jnp.int32, (sub, LANES), 1) < BLK

    def lane_tile(straight, crossed, s, t):
        parts = []
        for d in range(ADOM_DEV):
            slot = d * tiles + 2 * t
            first, second = block_of_ref[s, slot], block_of_ref[s, slot + 1]
            parts.append(jnp.where(low, straight[first], crossed[second]))
            parts.append(jnp.where(low, crossed[first], straight[second]))
        return jnp.concatenate(parts, 0)

    def wait_gather(step, carry):
        gather_copy(peer(step), peer(step)).wait_recv()
        return carry

    lax.fori_loop(0, n - 1, wait_gather, 0)

    to_scalars.wait()

    def add_y(s, state):
        acc_r, acc_l = state
        vec = trials[s].astype(BF16).astype(F32)
        for t in range(lane_tiles):
            tile = lane_tile(b_straight, b_crossed, s, t).astype(F32)
            acc_r = acc_r + tile * vec[t : t + 1, :]
            acc_l = acc_l + tile * vec[lane_tiles + t : lane_tiles + t + 1, :]
        return acc_r, acc_l

    zero = jnp.zeros((slab_rows, LANES), F32)
    acc_r, acc_l = lax.fori_loop(0, n, add_y, (zero, zero))
    y_ref[0] = jnp.broadcast_to(jnp.sum(acc_r, 1, keepdims=True), (slab_rows, LANES))
    y_ref[1] = jnp.broadcast_to(jnp.sum(acc_l, 1, keepdims=True), (slab_rows, LANES))

    per_occ = NVIR // pairs

    def columns(s):
        vec = trials[s].T
        return [
            jnp.concatenate(
                [
                    jnp.broadcast_to(vec[:, k : k + 1], (LANES, LANES))
                    for k in range(first, first + lane_tiles)
                ],
                0,
            )
            for first in (0, lane_tiles)
        ]

    def weights(s, cols, w_right, w_left, lane_tile_ids):
        shift = omega_ref[...] + 2.0 * occ_ref[s // per_occ]
        part = lax.rem(s, per_occ)
        column = vir_col[pl.ds(pl.multiple_of(part * pairs, pairs), pairs), :]
        energies = vir_ref[pl.ds(part * lane_tiles, lane_tiles), :]
        for t in lane_tile_ids:
            lanes = slice(t * LANES, (t + 1) * LANES)
            inverse = pl.reciprocal((shift - energies[t : t + 1, :]) - column, approx=True)
            w_right[:, lanes] = (inverse * cols[0]).astype(BF16)
            w_left[:, lanes] = (inverse * cols[1]).astype(BF16)

    def slab_term(s, w_right, w_left, later, later_right, later_left):
        b, x_r, x_l = [
            jnp.concatenate([lane_tile(straight, crossed, s, t) for t in range(lane_tiles)], 1)
            for _, _, straight, crossed in arrays
        ]
        stacked = jnp.concatenate([x_r, b], 0)
        cols = columns(later)
        for first in range(0, lane_tiles, PART):
            part = range(first, first + PART)
            lanes = slice(first * LANES, (first + PART) * LANES)
            weights(later, cols, later_right, later_left, part)
            both = jnp.dot(stacked, w_right[:, lanes], preferred_element_type=F32)
            t_r, t_b = both[:slab_rows], both[slab_rows:]
            t_l = jnp.dot(x_l, w_left[:, lanes], preferred_element_type=F32)
            y_r = jnp.concatenate([y_ref[0]] * PART, 1)
            y_l = jnp.concatenate([y_ref[1]] * PART, 1)
            b_part = b[:, lanes].astype(F32)
            sig_r = jnp.sum(
                b_part * (t_r + y_r) + x_r[:, lanes].astype(F32) * t_b, 0, keepdims=True
            )
            sig_l = jnp.sum(b_part * (t_l + y_l), 0, keepdims=True)
            for k, t in enumerate(part):
                lanes = slice(k * LANES, (k + 1) * LANES)
                share[s, t : t + 1, :] = sig_r[:, lanes]
                share[s, lane_tiles + t : lane_tiles + t + 1, :] = sig_l[:, lanes]

    weights(peer(0), columns(peer(0)), w_right0, w_left0, range(lane_tiles))

    def two_slabs(i, carry):
        now, then, after = peer(2 * i), peer(2 * i + 1), peer(2 * i + 2)
        slab_term(now, w_right0, w_left0, then, w_right1, w_left1)
        share_copy(now, me).start()
        slab_term(then, w_right1, w_left1, after, w_right0, w_left0)

        @pl.when(2 * i + 1 < n - 1)
        def _():
            share_copy(then, me).start()

        return carry

    lax.fori_loop(0, n // 2, two_slabs, 0)

    own = lax.rem(me, per_occ)
    energies = vir_ref[pl.ds(own * lane_tiles, lane_tiles), :] - occ_ref[me // per_occ]
    total = jnp.concatenate([energies, energies], 0) * trial_ref[...] + share[me]

    def collect(step, total):
        source = peer(step)
        share_copy(source, source).wait_recv()
        return total + arrived[source]

    out_ref[...] = lax.fori_loop(0, n - 1, collect, total)

    def wait_sent(step, carry):
        gather_copy(peer(step), me).wait_send()
        share_copy(peer(step), me).wait_send()
        return carry

    lax.fori_loop(0, n - 1, wait_sent, 0)


def on_device(
    blocks,
    right_xform,
    left_xform,
    owner,
    tile_slot,
    domain,
    live_count,
    right_vec,
    left_vec,
    occ_energy,
    vir_energy,
    omega,
):
    n = lax.axis_size("aux")
    nb_local, flat_width = blocks.shape
    pairs = right_vec.shape[0]
    lane_tiles = pairs // LANES
    vir = vir_energy.reshape(NVIR // LANES, LANES)
    sub = flat_width // LANES
    vmem, smem = (
        pl.BlockSpec(memory_space=pltpu.VMEM),
        pl.BlockSpec(memory_space=pltpu.SMEM),
    )
    out = pl.pallas_call(
        functools.partial(kernel, n),
        out_shape=jax.ShapeDtypeStruct((2 * lane_tiles, LANES), F32),
        in_specs=[smem] + [vmem] * 5 + [pl.BlockSpec(memory_space=pl.ANY)] * 3 + [vmem] * 3,
        out_specs=vmem,
        scratch_shapes=[
            *[pltpu.VMEM(blocks.shape, BF16)] * 3,
            pltpu.SemaphoreType.DMA((3,)),
            pltpu.VMEM((n, LANES), jnp.int32),
            pltpu.SMEM((n, LANES), jnp.int32),
            pltpu.SemaphoreType.DMA(()),
            pltpu.VMEM((2 * lane_tiles, LANES), F32),
            *[pltpu.VMEM((nb_local * (sub + 8), LANES), F32)] * 3,
            *[pltpu.VMEM((nb_local + 1, sub, LANES), BF16)] * 6,
            pltpu.VMEM((NVIR, LANES), F32),
            *[pltpu.VMEM((pairs, pairs), BF16)] * 4,
            pltpu.VMEM((2, ADOM_DEV * BLK, LANES), F32),
            pltpu.VMEM((n, 2 * lane_tiles, LANES), F32),
            pltpu.VMEM((n, 2 * lane_tiles, LANES), F32),
            pltpu.VMEM((n, 2 * lane_tiles, LANES), F32),
            pltpu.SemaphoreType.DMA((n,)),
            pltpu.SemaphoreType.DMA((n,)),
            pltpu.SemaphoreType.DMA((n,)),
            pltpu.SemaphoreType.DMA((n,)),
        ],
        compiler_params=pltpu.CompilerParams(
            collective_id=0, has_side_effects=True, vmem_limit_bytes=56 * 1024 * 1024
        ),
    )(
        occ_energy,
        omega.reshape(1, 1),
        live_count.reshape(1, 1),
        owner.reshape(1, nb_local),
        tile_slot.reshape(1, nb_local),
        domain.reshape(1, nb_local),
        blocks,
        right_xform,
        left_xform,
        right_vec.reshape(lane_tiles, LANES),
        left_vec.reshape(lane_tiles, LANES),
        vir,
    )
    return out[:lane_tiles].reshape(pairs), out[lane_tiles:].reshape(pairs)


def solution(mesh):
    in_specs = (
        P(("groups", "aux"), None),
        P(("groups", "aux"), None),
        P(("groups", "aux"), None),
        P(("groups", "aux"), None),
        P(("groups", "aux")),
        P(("groups", "aux")),
        P(("groups", "aux")),
        P(("groups", "aux")),
        P(("groups", "aux")),
        P("groups"),
        P("groups"),
        P("groups"),
    )
    out_specs = (P(("groups", "aux")), P(("groups", "aux")))
    return jax.shard_map(
        on_device, mesh=mesh, in_specs=in_specs, out_specs=out_specs, check_vma=False
    )
```

```python
import functools

import jax
import jax.numpy as jnp
from jax import lax
from jax.experimental import pallas as pl
from jax.experimental.pallas import tpu as pltpu
from jax.sharding import PartitionSpec as P

BLK = 64
NVIR = 2048
ADOM_DEV = 3
LANES = 128
WIDE = 8
PART = 2
F32 = jnp.float32
BF16 = jnp.bfloat16


def kernel(
    n,
    occ_ref,
    omega_ref,
    live_ref,
    owner_ref,
    slot_ref,
    domain_ref,
    blocks_hbm,
    right_hbm,
    left_hbm,
    right_vec_ref,
    left_vec_ref,
    vir_ref,
    out_ref,
    blocks_ref,
    right_ref,
    left_ref,
    load_sem,
    table,
    block_of_ref,
    table_sem,
    trial_ref,
    turned_b,
    turned_r,
    turned_l,
    b_straight,
    b_crossed,
    r_straight,
    r_crossed,
    l_straight,
    l_crossed,
    vir_col,
    w_right0,
    w_left0,
    w_right1,
    w_left1,
    y_ref,
    trials,
    share,
    arrived,
    gather_send,
    gather_recv,
    share_send,
    share_recv,
):
    me = lax.axis_index("aux")
    pairs = w_right0.shape[0]
    lane_tiles = pairs // LANES
    tiles = 2 * lane_tiles
    sub = BLK * BLK // LANES
    slab_rows = ADOM_DEV * BLK
    nb = blocks_ref.shape[0]
    pitch = turned_b.shape[0] // nb

    def peer(step):
        return lax.rem(me + 1 + step, n)

    barrier = pltpu.get_barrier_semaphore()

    def greet(step, carry):
        pl.semaphore_signal(barrier, inc=1, device_id={"aux": peer(step)})
        return carry

    loads = [
        pltpu.make_async_copy(source, target, load_sem.at[k])
        for k, (source, target) in enumerate(
            ((blocks_hbm, blocks_ref), (right_hbm, right_ref), (left_hbm, left_ref))
        )
    ]
    for load in loads:
        load.start()
    lax.fori_loop(0, n - 1, greet, 0)

    trial_ref[:lane_tiles, :] = right_vec_ref[...]
    trial_ref[lane_tiles:, :] = left_vec_ref[...]
    trials[me] = trial_ref[...]

    live = lax.broadcasted_iota(jnp.int32, (1, nb), 1) < live_ref[...]
    code = (owner_ref[...] * ADOM_DEV + domain_ref[...]) * tiles + slot_ref[...]
    code = jnp.where(live, code, -1).astype(F32)
    code_row = jnp.broadcast_to(code, (nb, nb))
    code_col = code_row.T
    same = jnp.where(code_col == code_row, 1.0, 0.0).astype(BF16)
    block_ids = lax.broadcasted_iota(jnp.int32, (nb, LANES), 0)
    lane_ids = lax.broadcasted_iota(jnp.int32, (nb, LANES), 1)

    def fill(s, carry):
        slots = (lane_ids + s * (ADOM_DEV * tiles)).astype(F32)
        held = jnp.where(code_col[:, :LANES] == slots, block_ids, nb)
        table[pl.ds(s, 1), :] = jnp.min(held, 0, keepdims=True)
        return carry

    lax.fori_loop(0, n, fill, 0)
    to_scalars = pltpu.make_async_copy(table, block_of_ref, table_sem)
    to_scalars.start()

    for i in range(NVIR // LANES):
        row = jnp.broadcast_to(vir_ref[i : i + 1, :], (LANES, LANES))
        vir_col[i * LANES : (i + 1) * LANES, :] = row.T

    def gather_copy(target, source):
        return pltpu.make_async_remote_copy(
            src_ref=trial_ref,
            dst_ref=trials.at[source],
            send_sem=gather_send.at[target],
            recv_sem=gather_recv.at[source],
            device_id={"aux": target},
        )

    def share_copy(target, source):
        return pltpu.make_async_remote_copy(
            src_ref=share.at[target],
            dst_ref=arrived.at[source],
            send_sem=share_send.at[target],
            recv_sem=share_recv.at[source],
            device_id={"aux": target},
        )

    def start_gather(step, carry):
        gather_copy(peer(step), me).start()
        return carry

    arrays = (
        (blocks_ref, turned_b, b_straight, b_crossed),
        (right_ref, turned_r, r_straight, r_crossed),
        (left_ref, turned_l, l_straight, l_crossed),
    )

    def merge(j, carry):
        first = pl.multiple_of(j * WIDE * LANES, WIDE * LANES)
        for source_ref, turned, _, _ in arrays:
            merged = jnp.dot(
                same, source_ref[:, pl.ds(first, WIDE * LANES)], preferred_element_type=F32
            )
            for k in range(WIDE):
                turned[pl.ds(j * WIDE + k, nb, stride=pitch), :] = merged[
                    :, k * LANES : (k + 1) * LANES
                ]
        return carry

    for load in loads:
        load.wait()
    lax.fori_loop(0, sub // WIDE, merge, 0)
    pl.semaphore_wait(barrier, n - 1)
    lax.fori_loop(0, n - 1, start_gather, 0)

    def settle(i, carry):
        for _, turned, straight, crossed in arrays:
            for k in range(16):
                b = i * 16 + k
                x = turned[pl.ds(pl.multiple_of(b * pitch, 8), sub), :]
                x = x.astype(BF16)
                straight[b] = x
                crossed[b] = jnp.concatenate([x[:, BLK:], x[:, :BLK]], 1)
        return carry

    lax.fori_loop(0, nb // 16, settle, 0)
    for _, _, straight, crossed in arrays:
        straight[nb] = jnp.zeros((sub, LANES), BF16)
        crossed[nb] = jnp.zeros((sub, LANES), BF16)

    low = lax.broadcasted_iota(jnp.int32, (sub, LANES), 1) < BLK

    def lane_tile(straight, crossed, s, t):
        parts = []
        for d in range(ADOM_DEV):
            slot = d * tiles + 2 * t
            first, second = block_of_ref[s, slot], block_of_ref[s, slot + 1]
            parts.append(jnp.where(low, straight[first], crossed[second]))
            parts.append(jnp.where(low, crossed[first], straight[second]))
        return jnp.concatenate(parts, 0)

    def wait_gather(step, carry):
        gather_copy(peer(step), peer(step)).wait_recv()
        return carry

    lax.fori_loop(0, n - 1, wait_gather, 0)

    to_scalars.wait()

    def add_y(s, state):
        acc_r, acc_l = state
        vec = trials[s].astype(BF16).astype(F32)
        for t in range(lane_tiles):
            tile = lane_tile(b_straight, b_crossed, s, t).astype(F32)
            acc_r = acc_r + tile * vec[t : t + 1, :]
            acc_l = acc_l + tile * vec[lane_tiles + t : lane_tiles + t + 1, :]
        return acc_r, acc_l

    zero = jnp.zeros((slab_rows, LANES), F32)
    acc_r, acc_l = lax.fori_loop(0, n, add_y, (zero, zero))
    y_ref[0] = jnp.broadcast_to(jnp.sum(acc_r, 1, keepdims=True), (slab_rows, LANES))
    y_ref[1] = jnp.broadcast_to(jnp.sum(acc_l, 1, keepdims=True), (slab_rows, LANES))

    per_occ = NVIR // pairs

    def columns(s):
        vec = trials[s].T
        return [
            jnp.concatenate(
                [
                    jnp.broadcast_to(vec[:, k : k + 1], (LANES, LANES))
                    for k in range(first, first + lane_tiles)
                ],
                0,
            )
            for first in (0, lane_tiles)
        ]

    def weights(s, cols, w_right, w_left, lane_tile_ids):
        shift = omega_ref[...] + 2.0 * occ_ref[s // per_occ]
        part = lax.rem(s, per_occ)
        column = vir_col[pl.ds(pl.multiple_of(part * pairs, pairs), pairs), :]
        energies = vir_ref[pl.ds(part * lane_tiles, lane_tiles), :]
        for t in lane_tile_ids:
            lanes = slice(t * LANES, (t + 1) * LANES)
            inverse = pl.reciprocal((shift - energies[t : t + 1, :]) - column, approx=True)
            w_right[:, lanes] = (inverse * cols[0]).astype(BF16)
            w_left[:, lanes] = (inverse * cols[1]).astype(BF16)

    def slab_term(s, w_right, w_left, later, later_right, later_left):
        b, x_r, x_l = [
            jnp.concatenate([lane_tile(straight, crossed, s, t) for t in range(lane_tiles)], 1)
            for _, _, straight, crossed in arrays
        ]
        stacked = jnp.concatenate([x_r, b], 0)
        cols = columns(later)
        for first in range(0, lane_tiles, PART):
            part = range(first, first + PART)
            lanes = slice(first * LANES, (first + PART) * LANES)
            weights(later, cols, later_right, later_left, part)
            both = jnp.dot(stacked, w_right[:, lanes], preferred_element_type=F32)
            t_r, t_b = both[:slab_rows], both[slab_rows:]
            t_l = jnp.dot(x_l, w_left[:, lanes], preferred_element_type=F32)
            y_r = jnp.concatenate([y_ref[0]] * PART, 1)
            y_l = jnp.concatenate([y_ref[1]] * PART, 1)
            b_part = b[:, lanes].astype(F32)
            sig_r = jnp.sum(
                b_part * (t_r + y_r) + x_r[:, lanes].astype(F32) * t_b, 0, keepdims=True
            )
            sig_l = jnp.sum(b_part * (t_l + y_l), 0, keepdims=True)
            for k, t in enumerate(part):
                lanes = slice(k * LANES, (k + 1) * LANES)
                share[s, t : t + 1, :] = sig_r[:, lanes]
                share[s, lane_tiles + t : lane_tiles + t + 1, :] = sig_l[:, lanes]

    weights(peer(0), columns(peer(0)), w_right0, w_left0, range(lane_tiles))

    def two_slabs(i, carry):
        now, then, after = peer(2 * i), peer(2 * i + 1), peer(2 * i + 2)
        slab_term(now, w_right0, w_left0, then, w_right1, w_left1)
        share_copy(now, me).start()
        slab_term(then, w_right1, w_left1, after, w_right0, w_left0)

        @pl.when(2 * i + 1 < n - 1)
        def _():
            share_copy(then, me).start()

        return carry

    lax.fori_loop(0, n // 2, two_slabs, 0)

    own = lax.rem(me, per_occ)
    energies = vir_ref[pl.ds(own * lane_tiles, lane_tiles), :] - occ_ref[me // per_occ]
    total = jnp.concatenate([energies, energies], 0) * trial_ref[...] + share[me]

    def collect(step, total):
        source = peer(step)
        share_copy(source, source).wait_recv()
        return total + arrived[source]

    out_ref[...] = lax.fori_loop(0, n - 1, collect, total)

    def wait_sent(step, carry):
        gather_copy(peer(step), me).wait_send()
        share_copy(peer(step), me).wait_send()
        return carry

    lax.fori_loop(0, n - 1, wait_sent, 0)


def on_device(
    blocks,
    right_xform,
    left_xform,
    owner,
    tile_slot,
    domain,
    live_count,
    right_vec,
    left_vec,
    occ_energy,
    vir_energy,
    omega,
):
    n = lax.axis_size("aux")
    nb_local, flat_width = blocks.shape
    pairs = right_vec.shape[0]
    lane_tiles = pairs // LANES
    vir = vir_energy.reshape(NVIR // LANES, LANES)
    sub = flat_width // LANES
    vmem, smem = (
        pl.BlockSpec(memory_space=pltpu.VMEM),
        pl.BlockSpec(memory_space=pltpu.SMEM),
    )
    out = pl.pallas_call(
        functools.partial(kernel, n),
        out_shape=jax.ShapeDtypeStruct((2 * lane_tiles, LANES), F32),
        in_specs=[smem] + [vmem] * 5 + [pl.BlockSpec(memory_space=pl.ANY)] * 3 + [vmem] * 3,
        out_specs=vmem,
        scratch_shapes=[
            *[pltpu.VMEM(blocks.shape, BF16)] * 3,
            pltpu.SemaphoreType.DMA((3,)),
            pltpu.VMEM((n, LANES), jnp.int32),
            pltpu.SMEM((n, LANES), jnp.int32),
            pltpu.SemaphoreType.DMA(()),
            pltpu.VMEM((2 * lane_tiles, LANES), F32),
            *[pltpu.VMEM((nb_local * (sub + 8), LANES), F32)] * 3,
            *[pltpu.VMEM((nb_local + 1, sub, LANES), BF16)] * 6,
            pltpu.VMEM((NVIR, LANES), F32),
            *[pltpu.VMEM((pairs, pairs), BF16)] * 4,
            pltpu.VMEM((2, ADOM_DEV * BLK, LANES), F32),
            pltpu.VMEM((n, 2 * lane_tiles, LANES), F32),
            pltpu.VMEM((n, 2 * lane_tiles, LANES), F32),
            pltpu.VMEM((n, 2 * lane_tiles, LANES), F32),
            pltpu.SemaphoreType.DMA((n,)),
            pltpu.SemaphoreType.DMA((n,)),
            pltpu.SemaphoreType.DMA((n,)),
            pltpu.SemaphoreType.DMA((n,)),
        ],
        compiler_params=pltpu.CompilerParams(
            collective_id=0, has_side_effects=True, vmem_limit_bytes=56 * 1024 * 1024
        ),
    )(
        occ_energy,
        omega.reshape(1, 1),
        live_count.reshape(1, 1),
        owner.reshape(1, nb_local),
        tile_slot.reshape(1, nb_local),
        domain.reshape(1, nb_local),
        blocks,
        right_xform,
        left_xform,
        right_vec.reshape(lane_tiles, LANES),
        left_vec.reshape(lane_tiles, LANES),
        vir,
    )
    return out[:lane_tiles].reshape(pairs), out[lane_tiles:].reshape(pairs)


def solution(mesh):
    in_specs = (
        P(("groups", "aux"), None),
        P(("groups", "aux"), None),
        P(("groups", "aux"), None),
        P(("groups", "aux"), None),
        P(("groups", "aux")),
        P(("groups", "aux")),
        P(("groups", "aux")),
        P(("groups", "aux")),
        P(("groups", "aux")),
        P("groups"),
        P("groups"),
        P("groups"),
    )
    out_specs = (P(("groups", "aux")), P(("groups", "aux")))
    return jax.shard_map(
        on_device, mesh=mesh, in_specs=in_specs, out_specs=out_specs, check_vma=False
    )
```

```python
import functools

import jax
import jax.numpy as jnp
from jax import lax
from jax.experimental import pallas as pl
from jax.experimental.pallas import tpu as pltpu
from jax.sharding import PartitionSpec as P

BLK = 64
NVIR = 2048
ADOM_DEV = 3
LANES = 128
WIDE = 8
PART = 2
F32 = jnp.float32
BF16 = jnp.bfloat16


def kernel(
    n,
    occ_ref,
    omega_ref,
    live_ref,
    owner_ref,
    slot_ref,
    domain_ref,
    blocks_hbm,
    right_hbm,
    left_hbm,
    right_vec_ref,
    left_vec_ref,
    vir_ref,
    out_ref,
    blocks_ref,
    right_ref,
    left_ref,
    load_sem,
    table,
    block_of_ref,
    table_sem,
    trial_ref,
    turned_b,
    turned_r,
    turned_l,
    b_straight,
    b_crossed,
    r_straight,
    r_crossed,
    l_straight,
    l_crossed,
    vir_col,
    w_right0,
    w_left0,
    w_right1,
    w_left1,
    y_ref,
    trials,
    share,
    arrived,
    gather_send,
    gather_recv,
    share_send,
    share_recv,
):
    me = lax.axis_index("aux")
    pairs = w_right0.shape[0]
    lane_tiles = pairs // LANES
    tiles = 2 * lane_tiles
    sub = BLK * BLK // LANES
    slab_rows = ADOM_DEV * BLK
    nb = blocks_ref.shape[0]
    pitch = turned_b.shape[0] // nb

    def peer(step):
        return lax.rem(me + 1 + step, n)

    barrier = pltpu.get_barrier_semaphore()

    def greet(step, carry):
        pl.semaphore_signal(barrier, inc=1, device_id={"aux": peer(step)})
        return carry

    loads = [
        pltpu.make_async_copy(source, target, load_sem.at[k])
        for k, (source, target) in enumerate(
            ((blocks_hbm, blocks_ref), (right_hbm, right_ref), (left_hbm, left_ref))
        )
    ]
    for load in loads:
        load.start()
    lax.fori_loop(0, n - 1, greet, 0)

    trial_ref[:lane_tiles, :] = right_vec_ref[...]
    trial_ref[lane_tiles:, :] = left_vec_ref[...]
    trials[me] = trial_ref[...]

    live = lax.broadcasted_iota(jnp.int32, (1, nb), 1) < live_ref[...]
    code = (owner_ref[...] * ADOM_DEV + domain_ref[...]) * tiles + slot_ref[...]
    code = jnp.where(live, code, -1).astype(F32)
    code_row = jnp.broadcast_to(code, (nb, nb))
    code_col = code_row.T
    same = jnp.where(code_col == code_row, 1.0, 0.0).astype(BF16)
    block_ids = lax.broadcasted_iota(jnp.int32, (nb, LANES), 0)
    lane_ids = lax.broadcasted_iota(jnp.int32, (nb, LANES), 1)

    def fill(s, carry):
        slots = (lane_ids + s * (ADOM_DEV * tiles)).astype(F32)
        held = jnp.where(code_col[:, :LANES] == slots, block_ids, nb)
        table[pl.ds(s, 1), :] = jnp.min(held, 0, keepdims=True)
        return carry

    lax.fori_loop(0, n, fill, 0)
    to_scalars = pltpu.make_async_copy(table, block_of_ref, table_sem)
    to_scalars.start()

    for i in range(NVIR // LANES):
        row = jnp.broadcast_to(vir_ref[i : i + 1, :], (LANES, LANES))
        vir_col[i * LANES : (i + 1) * LANES, :] = row.T

    def gather_copy(target, source):
        return pltpu.make_async_remote_copy(
            src_ref=trial_ref,
            dst_ref=trials.at[source],
            send_sem=gather_send.at[target],
            recv_sem=gather_recv.at[source],
            device_id={"aux": target},
        )

    def share_copy(target, source):
        return pltpu.make_async_remote_copy(
            src_ref=share.at[target],
            dst_ref=arrived.at[source],
            send_sem=share_send.at[target],
            recv_sem=share_recv.at[source],
            device_id={"aux": target},
        )

    def start_gather(step, carry):
        gather_copy(peer(step), me).start()
        return carry

    arrays = (
        (blocks_ref, turned_b, b_straight, b_crossed),
        (right_ref, turned_r, r_straight, r_crossed),
        (left_ref, turned_l, l_straight, l_crossed),
    )

    def merge(j, carry):
        first = pl.multiple_of(j * WIDE * LANES, WIDE * LANES)
        for source_ref, turned, _, _ in arrays:
            merged = jnp.dot(
                same, source_ref[:, pl.ds(first, WIDE * LANES)], preferred_element_type=F32
            )
            for k in range(WIDE):
                turned[pl.ds(j * WIDE + k, nb, stride=pitch), :] = merged[
                    :, k * LANES : (k + 1) * LANES
                ]
        return carry

    pl.semaphore_wait(barrier, n - 1)
    lax.fori_loop(0, n - 1, start_gather, 0)
    for load in loads:
        load.wait()
    lax.fori_loop(0, sub // WIDE, merge, 0)

    def settle(i, carry):
        for _, turned, straight, crossed in arrays:
            for k in range(16):
                b = i * 16 + k
                x = turned[pl.ds(pl.multiple_of(b * pitch, 8), sub), :]
                x = x.astype(BF16)
                straight[b] = x
                crossed[b] = jnp.concatenate([x[:, BLK:], x[:, :BLK]], 1)
        return carry

    lax.fori_loop(0, nb // 16, settle, 0)
    for _, _, straight, crossed in arrays:
        straight[nb] = jnp.zeros((sub, LANES), BF16)
        crossed[nb] = jnp.zeros((sub, LANES), BF16)

    low = lax.broadcasted_iota(jnp.int32, (sub, LANES), 1) < BLK

    def lane_tile(straight, crossed, s, t):
        parts = []
        for d in range(ADOM_DEV):
            slot = d * tiles + 2 * t
            first, second = block_of_ref[s, slot], block_of_ref[s, slot + 1]
            parts.append(jnp.where(low, straight[first], crossed[second]))
            parts.append(jnp.where(low, crossed[first], straight[second]))
        return jnp.concatenate(parts, 0)

    def wait_gather(step, carry):
        gather_copy(peer(step), peer(step)).wait_recv()
        return carry

    lax.fori_loop(0, n - 1, wait_gather, 0)

    to_scalars.wait()

    def add_y(s, state):
        acc_r, acc_l = state
        vec = trials[s].astype(BF16).astype(F32)
        for t in range(lane_tiles):
            tile = lane_tile(b_straight, b_crossed, s, t).astype(F32)
            acc_r = acc_r + tile * vec[t : t + 1, :]
            acc_l = acc_l + tile * vec[lane_tiles + t : lane_tiles + t + 1, :]
        return acc_r, acc_l

    zero = jnp.zeros((slab_rows, LANES), F32)
    acc_r, acc_l = lax.fori_loop(0, n, add_y, (zero, zero))
    y_ref[0] = jnp.broadcast_to(jnp.sum(acc_r, 1, keepdims=True), (slab_rows, LANES))
    y_ref[1] = jnp.broadcast_to(jnp.sum(acc_l, 1, keepdims=True), (slab_rows, LANES))

    per_occ = NVIR // pairs

    def columns(s):
        vec = trials[s].T
        return [
            jnp.concatenate(
                [
                    jnp.broadcast_to(vec[:, k : k + 1], (LANES, LANES))
                    for k in range(first, first + lane_tiles)
                ],
                0,
            )
            for first in (0, lane_tiles)
        ]

    def weights(s, cols, w_right, w_left, lane_tile_ids):
        shift = omega_ref[...] + 2.0 * occ_ref[s // per_occ]
        part = lax.rem(s, per_occ)
        column = vir_col[pl.ds(pl.multiple_of(part * pairs, pairs), pairs), :]
        energies = vir_ref[pl.ds(part * lane_tiles, lane_tiles), :]
        for t in lane_tile_ids:
            lanes = slice(t * LANES, (t + 1) * LANES)
            inverse = pl.reciprocal((shift - energies[t : t + 1, :]) - column, approx=True)
            w_right[:, lanes] = (inverse * cols[0]).astype(BF16)
            w_left[:, lanes] = (inverse * cols[1]).astype(BF16)

    def slab_term(s, w_right, w_left, later, later_right, later_left):
        b, x_r, x_l = [
            jnp.concatenate([lane_tile(straight, crossed, s, t) for t in range(lane_tiles)], 1)
            for _, _, straight, crossed in arrays
        ]
        stacked = jnp.concatenate([x_r, b], 0)
        cols = columns(later)
        for first in range(0, lane_tiles, PART):
            part = range(first, first + PART)
            lanes = slice(first * LANES, (first + PART) * LANES)
            weights(later, cols, later_right, later_left, part)
            both = jnp.dot(stacked, w_right[:, lanes], preferred_element_type=F32)
            t_r, t_b = both[:slab_rows], both[slab_rows:]
            t_l = jnp.dot(x_l, w_left[:, lanes], preferred_element_type=F32)
            y_r = jnp.concatenate([y_ref[0]] * PART, 1)
            y_l = jnp.concatenate([y_ref[1]] * PART, 1)
            b_part = b[:, lanes].astype(F32)
            sig_r = jnp.sum(
                b_part * (t_r + y_r) + x_r[:, lanes].astype(F32) * t_b, 0, keepdims=True
            )
            sig_l = jnp.sum(b_part * (t_l + y_l), 0, keepdims=True)
            for k, t in enumerate(part):
                lanes = slice(k * LANES, (k + 1) * LANES)
                share[s, t : t + 1, :] = sig_r[:, lanes]
                share[s, lane_tiles + t : lane_tiles + t + 1, :] = sig_l[:, lanes]

    weights(peer(0), columns(peer(0)), w_right0, w_left0, range(lane_tiles))

    def two_slabs(i, carry):
        now, then, after = peer(2 * i), peer(2 * i + 1), peer(2 * i + 2)
        slab_term(now, w_right0, w_left0, then, w_right1, w_left1)
        share_copy(now, me).start()
        slab_term(then, w_right1, w_left1, after, w_right0, w_left0)

        @pl.when(2 * i + 1 < n - 1)
        def _():
            share_copy(then, me).start()

        return carry

    lax.fori_loop(0, n // 2, two_slabs, 0)

    own = lax.rem(me, per_occ)
    energies = vir_ref[pl.ds(own * lane_tiles, lane_tiles), :] - occ_ref[me // per_occ]
    total = jnp.concatenate([energies, energies], 0) * trial_ref[...] + share[me]

    def collect(step, total):
        source = peer(step)
        share_copy(source, source).wait_recv()
        return total + arrived[source]

    out_ref[...] = lax.fori_loop(0, n - 1, collect, total)

    def wait_sent(step, carry):
        gather_copy(peer(step), me).wait_send()
        share_copy(peer(step), me).wait_send()
        return carry

    lax.fori_loop(0, n - 1, wait_sent, 0)


def on_device(
    blocks,
    right_xform,
    left_xform,
    owner,
    tile_slot,
    domain,
    live_count,
    right_vec,
    left_vec,
    occ_energy,
    vir_energy,
    omega,
):
    n = lax.axis_size("aux")
    nb_local, flat_width = blocks.shape
    pairs = right_vec.shape[0]
    lane_tiles = pairs // LANES
    vir = vir_energy.reshape(NVIR // LANES, LANES)
    sub = flat_width // LANES
    vmem, smem = (
        pl.BlockSpec(memory_space=pltpu.VMEM),
        pl.BlockSpec(memory_space=pltpu.SMEM),
    )
    out = pl.pallas_call(
        functools.partial(kernel, n),
        out_shape=jax.ShapeDtypeStruct((2 * lane_tiles, LANES), F32),
        in_specs=[smem] + [vmem] * 5 + [pl.BlockSpec(memory_space=pl.ANY)] * 3 + [vmem] * 3,
        out_specs=vmem,
        scratch_shapes=[
            *[pltpu.VMEM(blocks.shape, BF16)] * 3,
            pltpu.SemaphoreType.DMA((3,)),
            pltpu.VMEM((n, LANES), jnp.int32),
            pltpu.SMEM((n, LANES), jnp.int32),
            pltpu.SemaphoreType.DMA(()),
            pltpu.VMEM((2 * lane_tiles, LANES), F32),
            *[pltpu.VMEM((nb_local * (sub + 8), LANES), F32)] * 3,
            *[pltpu.VMEM((nb_local + 1, sub, LANES), BF16)] * 6,
            pltpu.VMEM((NVIR, LANES), F32),
            *[pltpu.VMEM((pairs, pairs), BF16)] * 4,
            pltpu.VMEM((2, ADOM_DEV * BLK, LANES), F32),
            pltpu.VMEM((n, 2 * lane_tiles, LANES), F32),
            pltpu.VMEM((n, 2 * lane_tiles, LANES), F32),
            pltpu.VMEM((n, 2 * lane_tiles, LANES), F32),
            pltpu.SemaphoreType.DMA((n,)),
            pltpu.SemaphoreType.DMA((n,)),
            pltpu.SemaphoreType.DMA((n,)),
            pltpu.SemaphoreType.DMA((n,)),
        ],
        compiler_params=pltpu.CompilerParams(
            collective_id=0, has_side_effects=True, vmem_limit_bytes=56 * 1024 * 1024
        ),
    )(
        occ_energy,
        omega.reshape(1, 1),
        live_count.reshape(1, 1),
        owner.reshape(1, nb_local),
        tile_slot.reshape(1, nb_local),
        domain.reshape(1, nb_local),
        blocks,
        right_xform,
        left_xform,
        right_vec.reshape(lane_tiles, LANES),
        left_vec.reshape(lane_tiles, LANES),
        vir,
    )
    return out[:lane_tiles].reshape(pairs), out[lane_tiles:].reshape(pairs)


def solution(mesh):
    in_specs = (
        P(("groups", "aux"), None),
        P(("groups", "aux"), None),
        P(("groups", "aux"), None),
        P(("groups", "aux"), None),
        P(("groups", "aux")),
        P(("groups", "aux")),
        P(("groups", "aux")),
        P(("groups", "aux")),
        P(("groups", "aux")),
        P("groups"),
        P("groups"),
        P("groups"),
    )
    out_specs = (P(("groups", "aux")), P(("groups", "aux")))
    return jax.shard_map(
        on_device, mesh=mesh, in_specs=in_specs, out_specs=out_specs, check_vma=False
    )
```
